32 devices in a mesh: dp: 8 (over y, x, core), mp: 4 (over z).
Axes of the slice: x: 2, y: 2, z: 4, core: 2. Of those that a mesh axis runs over, the one named last changes fastest.
Arguments:
- block_in: bfloat16 [8192, 1024], P('dp', 'mp'), may hold values from -6 to 6
- segments: int32 [8, 1024], P('dp'), may hold values from 0 to 3, never falling along the last dimension, each value on 1 to 800 neighbouring positions
- routes: int32 [8192, 8], P(('dp', 'mp')), may hold values from 0 to 31, all different within a row; in each aligned block of 256 rows (0 to 255, 256 to 511, ...) at most 96 rows name the same one
- attn_gain: float32 [1024], replicated, may hold values from 0.5 to 1.5
- w_query: bfloat16 [1024, 1024], P('dp', 'mp'), may hold values from -0.1875 to 0.1875
- w_key: bfloat16 [1024, 512], P('dp', 'mp'), may hold values from -0.1875 to 0.1875
- w_value: bfloat16 [1024, 512], P('dp', 'mp'), may hold values from -0.1875 to 0.1875
- w_out: bfloat16 [1024, 1024], P('dp', 'mp'), may hold values from -1.5 to 1.5
- moe_gain: float32 [1024], replicated, may hold values from 0.5 to 1.5
- w_router: bfloat16 [1024, 32], replicated, may hold values from -0.09375 to 0.09375
- w_gate_up: bfloat16 [32, 1024, 1024], P('dp', None, 'mp'), may hold values from -0.1875 to 0.1875
- w_down: bfloat16 [32, 512, 1024], P('dp', None, 'mp'), may hold values from -1 to 1
- grad_out: bfloat16 [8192, 1024], P(('dp', 'mp')), may hold values from -6 to 6
Outputs:
- block_out: bfloat16 [8192, 1024], P(('dp', 'mp'))
- grad_in: float32 [8192, 1024], P(('dp', 'mp'))
- grad_attn_gain: float32 [1024], replicated
- grad_w_query: float32 [1024, 1024], P('dp', 'mp')
- grad_w_key: float32 [1024, 512], P('dp', 'mp')
- grad_w_value: float32 [1024, 512], P('dp', 'mp')
- grad_w_out: float32 [1024, 1024], P('dp', 'mp')
- grad_moe_gain: float32 [1024], replicated
- grad_w_router: float32 [1024, 32], replicated
- grad_w_gate_up: float32 [32, 1024, 1024], P('dp', None, 'mp')
- grad_w_down: float32 [32, 512, 1024], P('dp', None, 'mp')
The draws below stay inside these ranges and needn't reach their ends.
Inputs may be any that keep to these rules, and one draw needn't show every extreme that they name: `routes`: each token names 8 different experts. Among the 256 rows of one device no expert is named more than 96 times, and some expert reaches 96 in some device's rows. `segments`: along each sequence the numbers never fall and start at 0; each document has 1 to 800 tokens, one exactly 800.
All inputs are finite; a program needn't handle non-finite values.
Results may differ from the reference program's by a relative error of at most 0.019.
Values may be sent and summed in bfloat16 or wider, within the bound.
A program may use at most 192 MiB of HBM per device.

```python
import math
import jax
import jax.numpy as jnp
import numpy as np
from jax import lax

D = 1024
H = 16
KVH = 8
HD = 64
EXPERTS = 32
FF = 512
TOPK = 8
LEN = 1024
DOCS = 4
TOK_DEV = 256
DOC_MOST = 800
SEQS = 8
TOKENS = 8192
CAP = 96
N_DP = 8
N_MP = 4


def levels(rng, extent, cuts, least, largest):
    def one(position, parts):
        steps = jax.random.uniform(jax.random.fold_in(jax.random.fold_in(rng, 6), position), (parts,), jnp.float32, least / len(cuts), largest / len(cuts))
        return jnp.repeat(jnp.exp(steps), extent[position] // parts).reshape((-1,) + (1,) * (len(extent) - position - 1))

    loudness = one(*cuts[0])
    for cut in cuts[1:]:
        loudness = loudness * one(*cut)
    return loudness


def length_profile(number_of, total, bound, lean):
    loads = [(1 << 20) // math.isqrt(standing ** lean) + 1 for standing in range(2, number_of + 1)]
    rest, holding = total - bound - (number_of - 1), [1] * (number_of - 1)
    while rest > 0:
        free = [i for i in range(number_of - 1) if holding[i] < bound]
        pool, left = sum([loads[i] for i in free]), rest
        for i in free:
            addition = min(bound - holding[i], max(1, left * loads[i] // pool), rest)
            holding[i] = holding[i] + addition
            rest = rest - addition
    return np.array([bound] + holding)


def uneven(key, number_of, total, bound, slope):
    if number_of == 2:
        one = jax.random.randint(key, (), max(1, total - bound), min(bound, total - 1) + 1)
        return jnp.stack([one, total - one])
    sizes = jnp.asarray(length_profile(number_of, total, bound, slope), jnp.int32)
    twos = (number_of - 1) // 2
    giver, taker = sizes[1:1 + 2 * twos:2], sizes[2:2 + 2 * twos:2]
    room = jnp.minimum(giver - 1, bound - taker)
    passed = jax.random.randint(jax.random.fold_in(key, 1), (twos,), 0, 1 << 20) % (room + 1)
    sizes = sizes.at[1:1 + 2 * twos:2].set(giver - passed).at[2:2 + 2 * twos:2].set(taker + passed)
    return sizes[jax.random.permutation(jax.random.fold_in(key, 2), number_of)]


def shared_out(stream_key, own, number, rows, number_of, top, bound, slope):
    ranking = jax.random.permutation(stream_key, number_of)
    crowded, ordinary = portions_of(number_of, rows * top, bound, slope, True), portions_of(number_of, rows * top, bound, slope, False)
    places = jnp.arange(number_of)

    def named(tallies, rotation):
        used = int((tallies > 0).sum())
        fixed = max(1, used // 4)
        passed = fixed + (places - fixed + rotation * (used - fixed)) % max(1, number_of - fixed)
        return jnp.zeros((number_of,), jnp.int32).at[ranking[jnp.where(places < fixed, places, passed)]].set(jnp.asarray(tallies, jnp.int32))

    tallies = jnp.where(number % 4 == 0, named(crowded, number // 4), named(ordinary, number - number // 4 - 1))
    mixed = jax.random.permutation(jax.random.fold_in(own, 3), number_of)
    giver, taker = mixed[0:number_of // 2 * 2:2], mixed[1:number_of // 2 * 2:2]
    room = jnp.minimum(tallies[giver] - 1, bound - tallies[taker]) // 2
    room = jnp.where((giver == ranking[0]) | (taker == ranking[0]) | (tallies[taker] == 0), 0, jnp.maximum(room, 0))
    passed = jax.random.randint(jax.random.fold_in(own, 4), (number_of // 2,), 0, 1 << 20) % (room + 1)
    tallies = tallies.at[giver].add(-passed).at[taker].add(passed)
    items = jnp.searchsorted(jnp.cumsum(tallies), jnp.arange(rows * top), side="right").astype(jnp.int32)
    grid = items.reshape(top, rows).T
    grid = grid[jax.random.permutation(jax.random.fold_in(own, 1), rows)]
    rotation = jax.random.randint(jax.random.fold_in(own, 2), (rows, 1), 0, top)
    return jnp.take_along_axis(grid, (jnp.arange(top)[None, :] + rotation) % top, axis=1)


def portions_of(count, total, bound, skew, full):
    portions = [(1 << 20) // math.isqrt(standing ** skew) + 1 for standing in range(1, count + 1)]
    largest = bound if full else min(bound, max(-(-total // count), total * portions[0] // sum(portions)))
    least = 1 if total - largest >= count - 1 else 0
    counts, rest = [largest] + [least] * (count - 1), total - largest - least * (count - 1)
    while rest > 0:
        movable = [i for i in range(1, count) if counts[i] < largest] or [i for i in range(1, count) if counts[i] < bound]
        pool, remaining = sum([portions[i] for i in movable]), rest
        for i in movable:
            addition = min(bound - counts[i], max(1, remaining * portions[i] // pool), rest)
            counts[i] = counts[i] + addition
            rest = rest - addition
    return np.array(counts)


def bell_draw(key, dims, deviation, reach, cuts=(), kind=jnp.bfloat16):
    loudness = levels(key, dims, cuts, -0.22, 0.18) if cuts else 1.0
    array = jax.random.normal(key, dims, jnp.float32) * deviation * loudness
    return jnp.minimum(jnp.maximum(array, -reach), reach).astype(kind)


def setup_inputs(seed: int = 0) -> dict:
    keys = jax.random.split(jax.random.key(seed), 14)
    block_in = bell_draw(keys[0], (TOKENS, D), 1.0, 6.0, ((0, 8), (1, 4)))
    segments = jax.vmap(lambda own: jnp.searchsorted(jnp.cumsum(uneven(own, DOCS, LEN, DOC_MOST, 0)), jnp.arange(LEN), side="right"))(jax.random.split(keys[1], SEQS)).reshape((SEQS, LEN)).astype(jnp.int32)
    routes_keys = jax.random.split(jax.random.fold_in(keys[2], 1), TOKENS // TOK_DEV)
    routes_turns = jax.random.permutation(jax.random.fold_in(keys[2], 3), TOKENS // TOK_DEV)
    routes = jax.vmap(lambda own, number: shared_out(jax.random.fold_in(keys[2], 2), own, number, TOK_DEV, EXPERTS, TOPK, CAP, 1))(routes_keys, routes_turns).reshape((TOKENS, TOPK))
    attn_gain = jnp.clip(1.0 + 0.1 * jax.random.normal(keys[3], (D,), jnp.float32), 0.5, 1.5)
    w_query = bell_draw(keys[4], (D, H * HD), D ** -0.5, 0.1875, ((0, 8), (1, 4)))
    w_key = bell_draw(keys[5], (D, KVH * HD), D ** -0.5, 0.1875, ((0, 8), (1, 4)))
    w_value = bell_draw(keys[6], (D, KVH * HD), D ** -0.5, 0.1875, ((0, 8), (1, 4)))
    w_out = bell_draw(keys[7], (D, H * HD), (H * HD // 64) ** -0.5, 1.5, ((0, 8), (1, 4)))
    moe_gain = jnp.clip(1.0 + 0.1 * jax.random.normal(keys[8], (D,), jnp.float32), 0.5, 1.5)
    w_router = bell_draw(keys[9], (D, EXPERTS), (0.5 * D ** -0.5), 0.09375)
    w_gate_up = bell_draw(keys[10], (EXPERTS, D, 2 * FF), D ** -0.5, 0.1875, ((0, 8), (2, 4)))
    w_down = bell_draw(keys[11], (EXPERTS, FF, D), (FF // 16) ** -0.5, 1.0, ((0, 8), (2, 4)))
    grad_out = bell_draw(keys[12], (TOKENS, D), 1.0, 6.0, ((0, 32),))
    return {"block_in": block_in, "segments": segments, "routes": routes, "attn_gain": attn_gain, "w_query": w_query, "w_key": w_key, "w_value": w_value, "w_out": w_out, "moe_gain": moe_gain, "w_router": w_router, "w_gate_up": w_gate_up, "w_down": w_down, "grad_out": grad_out}


EPS = 1e-06
ROPE_BASE = 10000.0
NEG_FILL = -1000000000.0
HIGH = lax.Precision.HIGHEST

@jax.custom_vjp
def low(v):
    return lax.optimization_barrier(v.astype(jnp.bfloat16)).astype(jnp.float32)

@jax.custom_vjp
def low_back(v):
    return v

def low_keep(v):
    return (low(v), None)

def low_pass(kept, grad):
    return (grad,)

def back_keep(v):
    return (v, None)

def back_low(kept, grad):
    return (low(grad),)
low.defvjp(low_keep, low_pass)
low_back.defvjp(back_keep, back_low)

def rms_scale(values, gain):
    return values * lax.rsqrt(lax.optimization_barrier(jnp.mean(values * values, axis=-1, keepdims=True)) + EPS) * gain

def positions_of(seg_row):
    index = jnp.arange(seg_row.shape[0], dtype=jnp.int32)
    change = jnp.concatenate([jnp.ones((1,), dtype=bool), seg_row[1:] != seg_row[:-1]])
    begin = lax.cummax(jnp.where(change, index, jnp.zeros_like(index)), axis=0)
    return index - begin

def angles(seg_row):
    place = positions_of(seg_row).astype(jnp.float32)
    freq = ROPE_BASE ** (-jnp.arange(0, HD, 2).astype(jnp.float32) / HD)
    theta = place[:, None] * freq[None, :]
    theta = jnp.concatenate([theta, theta], axis=1)
    return (jnp.cos(theta)[:, None, :], jnp.sin(theta)[:, None, :])

def rotate(values, cosine, sine):
    half = values.shape[-1] // 2
    turned = jnp.concatenate([-values[..., half:], values[..., :half]], axis=-1)
    return values * cosine + turned * sine

def allowed_pairs(seg_row):
    index = jnp.arange(seg_row.shape[0], dtype=jnp.int32)
    return (seg_row[:, None] == seg_row[None, :]) & (index[:, None] >= index[None, :])

def attend(packed):
    query, key, value, seg_row = packed
    cosine, sine = angles(seg_row)
    query_rot = low(rotate(query, cosine, sine))
    key_rot = low(rotate(key, cosine, sine))
    grouped = query_rot.reshape(LEN, KVH, H // KVH, HD)
    scores = jnp.einsum('qkgd,skd->kgqs', grouped, key_rot, precision=HIGH) * (1.0 / math.sqrt(HD))
    scores = low_back(scores)
    scores = jnp.where(allowed_pairs(seg_row), scores, NEG_FILL)
    probs = low(jax.nn.softmax(scores, axis=-1))
    mixed = jnp.einsum('kgqs,skd->qkgd', probs, value, precision=HIGH)
    return mixed.reshape(LEN, H * HD)

def reference(block_in, segments, routes, attn_gain, w_query, w_key, w_value, w_out, moe_gain, w_router, w_gate_up, w_down, grad_out):
    devices = N_DP * N_MP
    tokens = block_in.shape[0]
    seqs = segments.shape[0]
    dev_routes = routes.reshape(devices, TOK_DEV * TOPK)

    def ranks(row):
        onehot = (row[:, None] == jnp.arange(EXPERTS, dtype=jnp.int32)[None, :]).astype(jnp.int32)
        before = (jnp.cumsum(onehot, axis=0).astype(jnp.int32) - 1) * onehot
        return lax.optimization_barrier(jnp.sum(before, axis=1)).astype(jnp.int32)
    rank = lax.map(ranks, dev_routes)
    owner = jnp.arange(devices, dtype=jnp.int32)[:, None]
    slot = ((dev_routes * devices + owner) * CAP + rank).reshape(-1).astype(jnp.int32)
    source = jnp.repeat(jnp.arange(tokens, dtype=jnp.int32), TOPK)
    table = jnp.full((EXPERTS * devices * CAP,), tokens, dtype=jnp.int32).at[slot].set(source)
    table = table.reshape(EXPERTS, devices * CAP)

    def forward(stream, attn_g, wq, wk, wv, wo, moe_g, wr, wgu, wd):
        normed = low(rms_scale(stream, attn_g))
        query = low_back(jnp.dot(normed, wq, precision=HIGH))
        key = low_back(jnp.dot(normed, wk, precision=HIGH))
        value = low(low_back(jnp.dot(normed, wv, precision=HIGH)))
        heads = lax.map(jax.checkpoint(attend), (query.reshape(seqs, LEN, H, HD), key.reshape(seqs, LEN, KVH, HD), value.reshape(seqs, LEN, KVH, HD), segments))
        heads = low_back(low(heads.reshape(tokens, H * HD)))
        attn_mixed = low_back(jnp.dot(heads, wo.T, precision=HIGH))
        hidden = stream + attn_mixed
        moe_in = low(rms_scale(hidden, moe_g))
        logits = jnp.dot(moe_in, wr, precision=HIGH)
        gates = jax.nn.softmax(jnp.take_along_axis(logits, routes, axis=1), axis=1)
        padded = jnp.concatenate([moe_in, jnp.zeros((1, D), dtype=moe_in.dtype)], axis=0)

        def expert(packed):
            index, gate_up, down = packed
            rows = low_back(padded[index])
            both = low_back(jnp.dot(rows, gate_up, precision=HIGH))
            act = low(jax.nn.silu(both[:, :FF]) * both[:, FF:])
            return low_back(low(jnp.dot(act, down, precision=HIGH)))
        outputs = lax.map(jax.checkpoint(expert), (table, wgu, wd)).reshape(-1, D)
        chosen = outputs[slot].reshape(tokens, TOPK, D)
        return hidden + lax.optimization_barrier(jnp.sum(gates[:, :, None] * chosen, axis=1))
    floats = (block_in.astype(jnp.float32), attn_gain.astype(jnp.float32), w_query.astype(jnp.float32), w_key.astype(jnp.float32), w_value.astype(jnp.float32), w_out.astype(jnp.float32), moe_gain.astype(jnp.float32), w_router.astype(jnp.float32), w_gate_up.astype(jnp.float32), w_down.astype(jnp.float32))
    result, pullback = jax.vjp(forward, *floats)
    grads = pullback(grad_out.astype(jnp.float32))
    return (result.astype(jnp.bfloat16), grads[0], grads[1], grads[2], grads[3], grads[4], grads[5], grads[6], grads[7], grads[8], grads[9])
```

```python
import functools
import math

import jax
import jax.numpy as jnp
from jax import lax
from jax.experimental import pallas as pl
from jax.experimental.pallas import tpu as pltpu
from jax.sharding import PartitionSpec as P

D = 1024
HD = 64
EXPERTS = 32
FF = 512
TOPK = 8
CAP = 96


EPS = 1e-06
ROPE_BASE = 10000.0
NEG_FILL = -1000000000.0
HIGH = lax.Precision.HIGHEST


def rms_scale(values, gain):
    return values * lax.rsqrt(jnp.mean(values * values, axis=-1, keepdims=True) + EPS) * gain


def positions_of(seg_row):
    index = jnp.arange(seg_row.shape[0], dtype=jnp.int32)
    change = jnp.concatenate([jnp.ones((1,), dtype=bool), seg_row[1:] != seg_row[:-1]])
    begin = lax.cummax(jnp.where(change, index, jnp.zeros_like(index)), axis=0)
    return index - begin


def angles(seg_row):
    place = positions_of(seg_row).astype(jnp.float32)
    freq = ROPE_BASE ** (-jnp.arange(0, HD, 2).astype(jnp.float32) / HD)
    theta = place[:, None] * freq[None, :]
    theta = jnp.concatenate([theta, theta], axis=1)
    return (jnp.cos(theta)[:, None, :], jnp.sin(theta)[:, None, :])


def rotate(values, cosine, sine):
    half = values.shape[-1] // 2
    turned = jnp.concatenate([-values[..., half:], values[..., :half]], axis=-1)
    return values * cosine + turned * sine


def unrotate(values, cosine, sine):
    half = values.shape[-1] // 2
    spun = values * sine
    return values * cosine + jnp.concatenate([spun[..., half:], -spun[..., :half]], axis=-1)


def allowed_pairs(seg_row):
    index = jnp.arange(seg_row.shape[0], dtype=jnp.int32)
    return (seg_row[:, None] == seg_row[None, :]) & (index[:, None] >= index[None, :])


def attend_forward(packed):
    query, key, value, seg_row = packed
    length = seg_row.shape[0]
    cosine, sine = angles(seg_row)
    query_rot = rotate(query, cosine, sine).astype(jnp.bfloat16)
    key_rot = rotate(key, cosine, sine).astype(jnp.bfloat16)
    value_low = value.astype(jnp.bfloat16)
    grouped = query_rot.reshape(length, key.shape[1], -1, HD)
    scores = jnp.einsum("qkgd,skd->kgqs", grouped, key_rot, preferred_element_type=jnp.float32) * (
        1.0 / math.sqrt(HD)
    )
    scores = jnp.where(allowed_pairs(seg_row), scores, NEG_FILL)
    top_score = jnp.max(scores, axis=-1, keepdims=True)
    expos = jnp.exp(scores - top_score)
    totals = jnp.sum(expos, axis=-1, keepdims=True)
    probs_low = (expos / totals).astype(jnp.bfloat16)
    mixed = jnp.einsum("kgqs,skd->qkgd", probs_low, value_low, preferred_element_type=jnp.float32)
    log_total = top_score + jnp.log(totals)
    return (
        mixed.reshape(length, -1).astype(jnp.bfloat16),
        log_total,
        query_rot,
        key_rot,
        value_low,
    )


def attend_backward(packed):
    grad_mixed, query_rot, key_rot, value_low, log_total, seg_row = packed
    length = seg_row.shape[0]
    kv_heads = key_rot.shape[1]
    scale = 1.0 / math.sqrt(HD)
    grouped = query_rot.reshape(length, kv_heads, -1, HD)
    scores = (
        jnp.einsum("qkgd,skd->kgqs", grouped, key_rot, preferred_element_type=jnp.float32) * scale
    )
    scores = jnp.where(allowed_pairs(seg_row), scores, NEG_FILL)
    probs = jnp.exp(scores - log_total)
    grad_grouped = grad_mixed.reshape(length, kv_heads, -1, HD)
    grad_value = jnp.einsum(
        "kgqs,qkgd->skd",
        probs.astype(jnp.bfloat16),
        grad_grouped,
        preferred_element_type=jnp.float32,
    )
    grad_probs = jnp.einsum(
        "qkgd,skd->kgqs", grad_grouped, value_low, preferred_element_type=jnp.float32
    )
    centre = jnp.sum(probs * grad_probs, axis=-1, keepdims=True)
    grad_scores = (probs * (grad_probs - centre)).astype(jnp.bfloat16)
    grad_query = (
        jnp.einsum("kgqs,skd->qkgd", grad_scores, key_rot, preferred_element_type=jnp.float32)
        * scale
    )
    grad_key = (
        jnp.einsum("kgqs,qkgd->skd", grad_scores, grouped, preferred_element_type=jnp.float32)
        * scale
    )
    cosine, sine = angles(seg_row)
    grad_query = unrotate(grad_query.reshape(length, -1, HD), cosine, sine)
    grad_key = unrotate(grad_key, cosine, sine)
    return (
        grad_query.reshape(length, -1).astype(jnp.bfloat16),
        grad_key.reshape(length, -1).astype(jnp.bfloat16),
        grad_value.reshape(length, -1).astype(jnp.bfloat16),
    )


MESH = pl.DeviceIdType.MESH
VMEM_ASK = 56 * 1024 * 1024


def flip(index, bit):
    return index + bit - 2 * bit * ((index // bit) % 2)


def orders_of(size):
    bits = [1 << k for k in range(size.bit_length() - 1)]
    rest = bits[1:]
    cut = len(rest) // 2
    near, far = rest[:cut], rest[cut:]
    return [bits[:1] + near + far, bits[:1] + far + near]


def flip_any(index, mask):
    bit = 1
    while bit <= mask:
        if mask & bit:
            index = flip(index, bit)
        bit *= 2
    return index


def greet_cube(axis, me, size):
    barrier = pltpu.get_barrier_semaphore()
    bits = [1 << k for k in range(size.bit_length() - 1)]
    for bit in bits:
        pl.semaphore_signal(barrier, inc=1, device_id={axis: flip(me, bit)}, device_id_type=MESH)
    pl.semaphore_wait(barrier, len(bits))


def gather_kernel(axis, size, count, *refs):
    ins, outs, sems = refs[:count], refs[count : 2 * count], refs[2 * count :]
    me = lax.axis_index(axis)
    greet_cube(axis, me, size)
    for a in range(count):
        outs[a][me] = ins[a][...]
    orders = [order[::-1] for order in orders_of(size)]
    held = [[0], [0]]
    for phase in range(len(orders[0])):
        copies = []
        for a in range(count):
            half = ins[a].shape[0] // 2
            for part in range(2):
                bit = orders[part][phase]
                for mask in held[part]:
                    view = outs[a].at[flip_any(me, mask), pl.ds(part * half, half)]
                    copies.append(
                        pltpu.make_async_remote_copy(
                            src_ref=view,
                            dst_ref=view,
                            send_sem=sems[0].at[a, part, mask | bit],
                            recv_sem=sems[1].at[a, part, mask | bit],
                            device_id={axis: flip(me, bit)},
                            device_id_type=MESH,
                        )
                    )
        for copy in copies:
            copy.start()
        for copy in copies:
            copy.wait()
        held = [
            held[part] + [mask | orders[part][phase] for mask in held[part]] for part in range(2)
        ]


def params(number):
    return pltpu.CompilerParams(
        collective_id=number, has_side_effects=True, vmem_limit_bytes=VMEM_ASK
    )


def cost(byte_count):
    return pl.CostEstimate(flops=0, bytes_accessed=byte_count, transcendentals=0)


def cube_gather(arrays, axis, number):
    size = lax.axis_size(axis)
    count = len(arrays)
    return pl.pallas_call(
        functools.partial(gather_kernel, axis, size, count),
        out_shape=[jax.ShapeDtypeStruct((size,) + a.shape, a.dtype) for a in arrays],
        in_specs=[pl.BlockSpec(memory_space=pltpu.VMEM)] * count,
        out_specs=[pl.BlockSpec(memory_space=pltpu.VMEM)] * count,
        scratch_shapes=[pltpu.SemaphoreType.DMA((count, 2, size))] * 2,
        compiler_params=params(number),
        cost_estimate=cost(60000000),
        name="cube_gather",
    )(*arrays)


def scatter_kernel(axis, size, count, *refs):
    ins, outs = refs[:count], refs[count : 2 * count]
    got, keep = refs[2 * count : 3 * count], refs[3 * count : 4 * count]
    sems = refs[4 * count :]
    me = lax.axis_index(axis)
    greet_cube(axis, me, size)
    orders = orders_of(size)
    live = [list(range(size)), list(range(size))]
    phases = len(orders[0])
    for phase in range(phases):
        copies = []
        for a in range(count):
            half = outs[a].shape[0] // 2
            for part in range(2):
                bit = orders[part][phase]
                rows = pl.ds(part * half, half)
                for mask in live[part]:
                    if not mask & bit:
                        continue
                    if phase == 0:
                        source = ins[a].at[flip_any(me, mask), rows]
                    else:
                        source = keep[a].at[mask // 2, rows]
                    copies.append(
                        pltpu.make_async_remote_copy(
                            src_ref=source,
                            dst_ref=got[a].at[mask, rows],
                            send_sem=sems[0].at[a, part, mask],
                            recv_sem=sems[1].at[a, part, mask],
                            device_id={axis: flip(me, bit)},
                            device_id_type=MESH,
                        )
                    )
        for copy in copies:
            copy.start()
        for copy in copies:
            copy.wait()
        for a in range(count):
            half = outs[a].shape[0] // 2
            for part in range(2):
                bit = orders[part][phase]
                rows = pl.ds(part * half, half)
                stay = [mask for mask in live[part] if not mask & bit]
                for mask in stay:
                    if phase == 0:
                        own = ins[a][flip_any(me, mask), rows]
                    else:
                        own = keep[a][mask // 2, rows]
                    total = own.astype(jnp.float32) + got[a][mask | bit, rows].astype(jnp.float32)
                    if phase == phases - 1:
                        outs[a][rows] = total
                    else:
                        keep[a][mask // 2, rows] = total.astype(keep[a].dtype)
        live = [[m for m in live[part] if not m & orders[part][phase]] for part in range(2)]


def cube_scatter(arrays, axis, number):
    size = lax.axis_size(axis)
    count = len(arrays)
    slots = [pltpu.VMEM(a.shape, a.dtype) for a in arrays]
    return pl.pallas_call(
        functools.partial(scatter_kernel, axis, size, count),
        out_shape=[jax.ShapeDtypeStruct(a.shape[1:], jnp.float32) for a in arrays],
        in_specs=[pl.BlockSpec(memory_space=pltpu.VMEM)] * count,
        out_specs=[pl.BlockSpec(memory_space=pltpu.VMEM)] * count,
        scratch_shapes=slots
        + [pltpu.VMEM((size // 2,) + a.shape[1:], a.dtype) for a in arrays]
        + [pltpu.SemaphoreType.DMA((count, 2, size))] * 2,
        compiler_params=params(number),
        cost_estimate=cost(60000000),
        name="cube_scatter",
    )(*arrays)


def greet_line(axis, me, size):
    barrier = pltpu.get_barrier_semaphore()
    for ok, other in ((me < size - 1, me + 1), (me > 0, me - 1)):

        @pl.when(ok)
        def _(other=other):
            pl.semaphore_signal(barrier, inc=1, device_id={axis: other}, device_id_type=MESH)

    inner = (me < size - 1) & (me > 0)

    @pl.when(inner)
    def _():
        pl.semaphore_wait(barrier, 2)

    @pl.when(jnp.logical_not(inner))
    def _():
        pl.semaphore_wait(barrier, 1)


def line_gather_kernel(axis, size, x_ref, out_ref, send_sem, recv_sem):
    me = lax.axis_index(axis)
    greet_line(axis, me, size)
    out_ref[me] = x_ref[...]

    def copy_of(way, step, block, target):
        return pltpu.make_async_remote_copy(
            src_ref=out_ref.at[block],
            dst_ref=out_ref.at[block],
            send_sem=send_sem.at[way, step],
            recv_sem=recv_sem.at[way, step],
            device_id={axis: target},
            device_id_type=MESH,
        )

    for step in range(size - 1):

        @pl.when((me - step >= 0) & (me < size - 1))
        def _(step=step):
            copy_of(0, step, me - step, me + 1).start()

        @pl.when((me + step <= size - 1) & (me > 0))
        def _(step=step):
            copy_of(1, step, me + step, me - 1).start()

        @pl.when(me - 1 - step >= 0)
        def _(step=step):
            copy_of(0, step, me - 1 - step, me - 1).wait_recv()

        @pl.when(me + 1 + step <= size - 1)
        def _(step=step):
            copy_of(1, step, me + 1 + step, me + 1).wait_recv()

    for step in range(size - 1):

        @pl.when((me - step >= 0) & (me < size - 1))
        def _(step=step):
            copy_of(0, step, me - step, me + 1).wait_send()

        @pl.when((me + step <= size - 1) & (me > 0))
        def _(step=step):
            copy_of(1, step, me + step, me - 1).wait_send()


def line_gather(array, axis, number):
    size = lax.axis_size(axis)
    return pl.pallas_call(
        functools.partial(line_gather_kernel, axis, size),
        out_shape=jax.ShapeDtypeStruct((size,) + array.shape, array.dtype),
        in_specs=[pl.BlockSpec(memory_space=pltpu.VMEM)],
        out_specs=pl.BlockSpec(memory_space=pltpu.VMEM),
        scratch_shapes=[pltpu.SemaphoreType.DMA((2, size))] * 2,
        compiler_params=params(number),
        cost_estimate=cost(80000000),
        name="line_gather",
    )(array)


def line_scatter_kernel(axis, size, x_ref, out_ref, stage, got, send_sem, recv_sem):
    me = lax.axis_index(axis)
    greet_line(axis, me, size)

    def copy_of(way, dest, target):
        return pltpu.make_async_remote_copy(
            src_ref=stage.at[way, dest],
            dst_ref=got.at[way, dest],
            send_sem=send_sem.at[way, dest],
            recv_sem=recv_sem.at[way, dest],
            device_id={axis: target},
            device_id_type=MESH,
        )

    def pass_on(way, dest, source, target, first):
        @pl.when(first)
        def _():
            stage[way, dest] = x_ref[dest]

        @pl.when(jnp.logical_not(first))
        def _():
            copy_of(way, dest, source).wait_recv()
            stage[way, dest] = (
                x_ref[dest].astype(jnp.float32) + got[way, dest].astype(jnp.float32)
            ).astype(stage.dtype)

        copy_of(way, dest, target).start()

    for k in range(size - 1):
        up, down = size - 1 - k, k

        @pl.when(me < up)
        def _(up=up):
            pass_on(0, up, me - 1, me + 1, me == 0)

        @pl.when(me > down)
        def _(down=down):
            pass_on(1, down, me + 1, me - 1, me == size - 1)

    out_ref[...] = x_ref[me].astype(jnp.float32)

    @pl.when(me > 0)
    def _():
        copy_of(0, me, me - 1).wait_recv()
        out_ref[...] += got[0, me].astype(jnp.float32)

    @pl.when(me < size - 1)
    def _():
        copy_of(1, me, me + 1).wait_recv()
        out_ref[...] += got[1, me].astype(jnp.float32)

    for k in range(size - 1):
        up, down = size - 1 - k, k

        @pl.when(me < up)
        def _(up=up):
            copy_of(0, up, me + 1).wait_send()

        @pl.when(me > down)
        def _(down=down):
            copy_of(1, down, me - 1).wait_send()


def line_scatter(array, axis, number):
    size = lax.axis_size(axis)
    return pl.pallas_call(
        functools.partial(line_scatter_kernel, axis, size),
        out_shape=jax.ShapeDtypeStruct(array.shape[1:], jnp.float32),
        in_specs=[pl.BlockSpec(memory_space=pltpu.VMEM)],
        out_specs=pl.BlockSpec(memory_space=pltpu.VMEM),
        scratch_shapes=[pltpu.VMEM((2,) + array.shape, array.dtype)] * 2
        + [pltpu.SemaphoreType.DMA((2, size))] * 2,
        compiler_params=params(number),
        cost_estimate=cost(80000000),
        name="line_scatter",
    )(array)


def total_kernel(sizes, x_ref, out_ref, got, sent, send_sem, recv_sem):
    steps = []
    for axis, size in sizes:
        steps += [(axis, 1 << k) for k in range(size.bit_length() - 1)]
    barrier = pltpu.get_barrier_semaphore()
    for axis, bit in steps:
        pl.semaphore_signal(
            barrier,
            inc=1,
            device_id={axis: flip(lax.axis_index(axis), bit)},
            device_id_type=MESH,
        )
    pl.semaphore_wait(barrier, len(steps))
    sent[0] = x_ref[...]
    for k, (axis, bit) in enumerate(steps):
        copy = pltpu.make_async_remote_copy(
            src_ref=sent.at[k],
            dst_ref=got.at[k],
            send_sem=send_sem.at[k],
            recv_sem=recv_sem.at[k],
            device_id={axis: flip(lax.axis_index(axis), bit)},
            device_id_type=MESH,
        )
        copy.start()
        copy.wait()
        if k == len(steps) - 1:
            out_ref[...] = sent[k] + got[k]
        else:
            sent[k + 1] = sent[k] + got[k]


def total_of(array, axes, number):
    sizes = [(axis, lax.axis_size(axis)) for axis in axes]
    count = sum(size.bit_length() - 1 for _, size in sizes)
    return pl.pallas_call(
        functools.partial(total_kernel, sizes),
        out_shape=jax.ShapeDtypeStruct(array.shape, array.dtype),
        in_specs=[pl.BlockSpec(memory_space=pltpu.VMEM)],
        out_specs=pl.BlockSpec(memory_space=pltpu.VMEM),
        scratch_shapes=[pltpu.VMEM((count,) + array.shape, array.dtype)] * 2
        + [pltpu.SemaphoreType.DMA((count,))] * 2,
        compiler_params=params(number),
        cost_estimate=cost(60000000),
        name="total",
    )(array)


def local(
    block_in,
    segments,
    routes,
    attn_gain,
    w_query,
    w_key,
    w_value,
    w_out,
    moe_gain,
    w_router,
    w_gate_up,
    w_down,
    grad_out,
):
    dp_size = lax.axis_size("dp")
    mp_index = lax.axis_index("mp")
    dp_index = lax.axis_index("dp")
    tok_dev = routes.shape[0]
    seqs_here = segments.shape[0]
    exp_dev = EXPERTS // dp_size
    gate_up = lax.all_gather(w_gate_up, "mp", axis=2, tiled=True)
    down_full = lax.all_gather(w_down, "mp", axis=2, tiled=True)
    stacked = line_gather(block_in, "mp", 1)
    full_rows = stacked.transpose(1, 0, 2).reshape(block_in.shape[0], -1)
    row_count = full_rows.shape[0]
    length = row_count // seqs_here
    wide = full_rows.astype(jnp.float32)
    normed_low = rms_scale(wide, attn_gain).astype(jnp.bfloat16)
    q_cols, k_cols = w_query.shape[1], w_key.shape[1]
    packed = jnp.concatenate([w_query, w_key, w_value, w_out], axis=1)
    (gathered,) = cube_gather([packed], "dp", 2)
    gathered = gathered.reshape(-1, packed.shape[1])
    qkv_cols = q_cols + 2 * k_cols
    qkv_full = gathered[:, :qkv_cols]
    out_part = gathered[:, qkv_cols:]
    qkv = jnp.dot(normed_low, qkv_full, preferred_element_type=jnp.float32)
    query = qkv[:, :q_cols]
    key = qkv[:, q_cols : q_cols + k_cols]
    value = qkv[:, q_cols + k_cols :]
    head_local = q_cols // HD
    kv_local = k_cols // HD
    mixed, log_total, query_rot, key_rot, value_low = lax.map(
        attend_forward,
        (
            query.reshape(seqs_here, length, head_local, HD),
            key.reshape(seqs_here, length, kv_local, HD),
            value.reshape(seqs_here, length, kv_local, HD),
            segments,
        ),
    )
    heads_low = mixed.reshape(row_count, head_local * HD)
    row_start = mp_index * tok_dev
    attn_mixed = line_scatter(
        jnp.einsum("rh,dh->rd", heads_low, out_part, preferred_element_type=jnp.float32)
        .astype(jnp.bfloat16)
        .reshape(-1, tok_dev, D),
        "mp",
        3,
    )
    own_rows = lax.dynamic_slice_in_dim(wide, row_start, tok_dev, 0)
    hidden = own_rows + attn_mixed
    moe_low = rms_scale(hidden, moe_gain).astype(jnp.bfloat16)
    logits = jnp.dot(moe_low, w_router, preferred_element_type=jnp.float32)
    used = jnp.sum(
        (routes[:, :, None] == jnp.arange(EXPERTS, dtype=jnp.int32)[None, None, :]).astype(
            jnp.float32
        ),
        axis=1,
    )
    routed = used > 0.0
    top_logit = jnp.max(jnp.where(routed, logits, NEG_FILL), axis=1, keepdims=True)
    raised = jnp.where(routed, jnp.exp(jnp.where(routed, logits - top_logit, 0.0)), 0.0)
    gates = raised / jnp.sum(raised, axis=1, keepdims=True)
    order = jnp.arange(tok_dev, dtype=jnp.int32)
    before = (order[:, None] > order[None, :]).astype(jnp.bfloat16)
    rank = jnp.dot(before, used.astype(jnp.bfloat16), preferred_element_type=jnp.float32)
    rank = jnp.where(routed, rank, -1.0)
    info = jnp.concatenate(
        [gates, rank, jnp.zeros((tok_dev, 128 - 2 * EXPERTS), jnp.float32)], axis=1
    )
    tokens, tops, infos = cube_gather([moe_low, grad_out, info], "dp", 4)
    first = dp_index * exp_dev
    gate_cols = lax.dynamic_slice_in_dim(infos, first, exp_dev, 2)
    rank_cols = lax.dynamic_slice_in_dim(infos, EXPERTS + first, exp_dev, 2)
    gate_cols = gate_cols.transpose(0, 2, 1)
    rank_cols = rank_cols.transpose(0, 2, 1)
    place = jnp.arange(CAP, dtype=jnp.float32)[None, None, :, None]
    picks_wide = rank_cols[:, :, None, :] == place
    picks = picks_wide.astype(jnp.bfloat16)
    slot_gates = jnp.sum(jnp.where(picks_wide, gate_cols[:, :, None, :], 0.0), axis=3)
    arrived = jnp.einsum(
        "sect,std->secd", picks, tokens, preferred_element_type=jnp.float32
    ).astype(jnp.bfloat16)
    top_rows = jnp.einsum("sect,std->secd", picks, tops, preferred_element_type=jnp.float32)
    grad_arrived = (slot_gates[..., None] * top_rows).astype(jnp.bfloat16)
    both = jnp.einsum("secd,edf->secf", arrived, gate_up, preferred_element_type=jnp.float32)
    gate_part = both[..., :FF]
    up_part = both[..., FF:]
    act_low = (jax.nn.silu(gate_part) * up_part).astype(jnp.bfloat16)
    expert_out = jnp.einsum(
        "secf,efd->secd", act_low, down_full, preferred_element_type=jnp.float32
    ).astype(jnp.bfloat16)
    grad_slots = jnp.sum(top_rows * expert_out.astype(jnp.float32), axis=3)
    scaled_out = (slot_gates[..., None] * expert_out.astype(jnp.float32)).astype(jnp.bfloat16)
    part_out = jnp.einsum(
        "sect,secd->std", picks, scaled_out, preferred_element_type=jnp.float32
    ).astype(jnp.bfloat16)
    grad_act = jnp.einsum(
        "secd,efd->secf", grad_arrived, down_full, preferred_element_type=jnp.float32
    )
    grad_down = jnp.einsum(
        "secf,secd->efd", act_low, grad_arrived, preferred_element_type=jnp.float32
    )
    grad_down = lax.psum_scatter(
        grad_down.astype(jnp.bfloat16), "mp", scatter_dimension=2, tiled=True
    ).astype(jnp.float32)
    sigma = jax.nn.sigmoid(gate_part)
    grad_gate = grad_act * up_part * sigma * (1.0 + gate_part * (1.0 - sigma))
    grad_up = grad_act * gate_part * sigma
    grad_both = jnp.concatenate([grad_gate, grad_up], axis=-1).astype(jnp.bfloat16)
    grad_gate_up = jnp.einsum(
        "secd,secf->edf", arrived, grad_both, preferred_element_type=jnp.float32
    )
    grad_gate_up = lax.psum_scatter(
        grad_gate_up.astype(jnp.bfloat16), "mp", scatter_dimension=2, tiled=True
    ).astype(jnp.float32)
    grad_copy = jnp.einsum(
        "secf,edf->secd", grad_both, gate_up, preferred_element_type=jnp.float32
    ).astype(jnp.bfloat16)
    part_moe = jnp.einsum(
        "sect,secd->std", picks, grad_copy, preferred_element_type=jnp.float32
    ).astype(jnp.bfloat16)
    part_gates = jnp.sum(jnp.where(picks_wide, grad_slots[..., None], 0.0), axis=2)
    part_gates = lax.dynamic_update_slice_in_dim(
        jnp.zeros((dp_size, tok_dev, 128), jnp.float32), part_gates.transpose(0, 2, 1), first, 2
    )
    moe_sum, grad_gates = cube_scatter([part_moe, part_gates], "dp", 5)
    (out_sum,) = cube_scatter([part_out], "dp", 6)
    block_out = (hidden + out_sum).astype(jnp.bfloat16)
    grad_gates = grad_gates[:, :EXPERTS]
    grad_top = grad_out.astype(jnp.float32)
    grad_logits = gates * (grad_gates - jnp.sum(gates * grad_gates, axis=1, keepdims=True))
    router_wide = w_router.astype(jnp.float32)
    grad_moe = moe_sum + jnp.einsum("te,de->td", grad_logits, router_wide, precision=HIGH)
    grad_router = jnp.einsum("td,te->ed", moe_low.astype(jnp.float32), grad_logits, precision=HIGH)
    unused, moe_pull = jax.vjp(rms_scale, hidden, moe_gain)
    grad_hidden, grad_moe_gain = moe_pull(grad_moe)
    grad_hidden = grad_hidden + grad_top
    grad_hidden_low = grad_hidden.astype(jnp.bfloat16)
    grad_full = line_gather(grad_hidden_low, "mp", 7).reshape(row_count, D)
    grad_heads = jnp.dot(grad_full, out_part, preferred_element_type=jnp.float32).astype(
        jnp.bfloat16
    )
    grad_out_w = jnp.einsum("rd,rh->dh", grad_full, heads_low, preferred_element_type=jnp.float32)
    grad_query, grad_key, grad_value = lax.map(
        attend_backward,
        (
            grad_heads.reshape(seqs_here, length, head_local * HD),
            query_rot,
            key_rot,
            value_low,
            log_total,
            segments,
        ),
    )
    grad_qkv = jnp.concatenate(
        [
            grad_query.reshape(row_count, q_cols),
            grad_key.reshape(row_count, k_cols),
            grad_value.reshape(row_count, k_cols),
        ],
        axis=1,
    )
    grad_normed = line_scatter(
        jnp.einsum("rh,dh->rd", grad_qkv, qkv_full, preferred_element_type=jnp.float32)
        .astype(jnp.bfloat16)
        .reshape(-1, tok_dev, D),
        "mp",
        8,
    )
    unused_two, attn_pull = jax.vjp(rms_scale, own_rows, attn_gain)
    grad_own, grad_attn_gain = attn_pull(grad_normed)
    grad_in = grad_own + grad_hidden
    grad_qkv_w = jnp.einsum("rd,rh->dh", normed_low, grad_qkv, preferred_element_type=jnp.float32)
    grad_w = jnp.concatenate([grad_qkv_w, grad_out_w], axis=1).astype(jnp.bfloat16)
    (grad_w,) = cube_scatter([grad_w.reshape(dp_size, -1, grad_w.shape[1])], "dp", 9)
    small = jnp.concatenate(
        [
            grad_router,
            grad_attn_gain[None, :],
            grad_moe_gain[None, :],
            jnp.zeros((6, D), jnp.float32),
        ],
        axis=0,
    )
    small = total_of(small, ("dp", "mp"), 10)
    return (
        block_out,
        grad_in,
        small[EXPERTS],
        grad_w[:, :q_cols],
        grad_w[:, q_cols : q_cols + k_cols],
        grad_w[:, q_cols + k_cols : qkv_cols],
        grad_w[:, qkv_cols:],
        small[EXPERTS + 1],
        small[:EXPERTS].T,
        grad_gate_up,
        grad_down,
    )


def solution(mesh):
    placed = (
        P("dp", "mp"),
        P("dp", None),
        P(("dp", "mp"), None),
        P(),
        P("dp", "mp"),
        P("dp", "mp"),
        P("dp", "mp"),
        P("dp", "mp"),
        P(),
        P(),
        P("dp", None, "mp"),
        P("dp", None, "mp"),
        P(("dp", "mp"), None),
    )
    return jax.shard_map(
        local,
        mesh=mesh,
        in_specs=placed,
        out_specs=(
            P(("dp", "mp"), None),
            P(("dp", "mp"), None),
            P(),
            P("dp", "mp"),
            P("dp", "mp"),
            P("dp", "mp"),
            P("dp", "mp"),
            P(),
            P(),
            P("dp", None, "mp"),
            P("dp", None, "mp"),
        ),
        check_vma=False,
    )
```

```python
import functools
import math

import jax
import jax.numpy as jnp
from jax import lax
from jax.experimental import pallas as pl
from jax.experimental.pallas import tpu as pltpu
from jax.sharding import PartitionSpec as P

D = 1024
HD = 64
EXPERTS = 32
FF = 512
TOPK = 8
CAP = 96


EPS = 1e-06
ROPE_BASE = 10000.0
NEG_FILL = -1000000000.0
HIGH = lax.Precision.HIGHEST


def rms_scale(values, gain):
    return values * lax.rsqrt(jnp.mean(values * values, axis=-1, keepdims=True) + EPS) * gain


def positions_of(seg_row):
    index = jnp.arange(seg_row.shape[0], dtype=jnp.int32)
    change = jnp.concatenate([jnp.ones((1,), dtype=bool), seg_row[1:] != seg_row[:-1]])
    begin = lax.cummax(jnp.where(change, index, jnp.zeros_like(index)), axis=0)
    return index - begin


def angles(seg_row):
    place = positions_of(seg_row).astype(jnp.float32)
    freq = ROPE_BASE ** (-jnp.arange(0, HD, 2).astype(jnp.float32) / HD)
    theta = place[:, None] * freq[None, :]
    theta = jnp.concatenate([theta, theta], axis=1)
    return (jnp.cos(theta)[:, None, :], jnp.sin(theta)[:, None, :])


def rotate(values, cosine, sine):
    half = values.shape[-1] // 2
    turned = jnp.concatenate([-values[..., half:], values[..., :half]], axis=-1)
    return values * cosine + turned * sine


def unrotate(values, cosine, sine):
    half = values.shape[-1] // 2
    spun = values * sine
    return values * cosine + jnp.concatenate([spun[..., half:], -spun[..., :half]], axis=-1)


def allowed_pairs(seg_row):
    index = jnp.arange(seg_row.shape[0], dtype=jnp.int32)
    return (seg_row[:, None] == seg_row[None, :]) & (index[:, None] >= index[None, :])


def attend_forward(packed):
    query, key, value, seg_row = packed
    length = seg_row.shape[0]
    cosine, sine = angles(seg_row)
    query_rot = rotate(query, cosine, sine).astype(jnp.bfloat16)
    key_rot = rotate(key, cosine, sine).astype(jnp.bfloat16)
    value_low = value.astype(jnp.bfloat16)
    grouped = query_rot.reshape(length, key.shape[1], -1, HD)
    scores = jnp.einsum("qkgd,skd->kgqs", grouped, key_rot, preferred_element_type=jnp.float32) * (
        1.0 / math.sqrt(HD)
    )
    scores = jnp.where(allowed_pairs(seg_row), scores, NEG_FILL)
    top_score = jnp.max(scores, axis=-1, keepdims=True)
    expos = jnp.exp(scores - top_score)
    totals = jnp.sum(expos, axis=-1, keepdims=True)
    probs_low = (expos / totals).astype(jnp.bfloat16)
    mixed = jnp.einsum("kgqs,skd->qkgd", probs_low, value_low, preferred_element_type=jnp.float32)
    log_total = top_score + jnp.log(totals)
    return (
        mixed.reshape(length, -1).astype(jnp.bfloat16),
        log_total,
        query_rot,
        key_rot,
        value_low,
    )


def attend_backward(packed):
    grad_mixed, query_rot, key_rot, value_low, log_total, seg_row = packed
    length = seg_row.shape[0]
    kv_heads = key_rot.shape[1]
    scale = 1.0 / math.sqrt(HD)
    grouped = query_rot.reshape(length, kv_heads, -1, HD)
    scores = (
        jnp.einsum("qkgd,skd->kgqs", grouped, key_rot, preferred_element_type=jnp.float32) * scale
    )
    scores = jnp.where(allowed_pairs(seg_row), scores, NEG_FILL)
    probs = jnp.exp(scores - log_total)
    grad_grouped = grad_mixed.reshape(length, kv_heads, -1, HD)
    grad_value = jnp.einsum(
        "kgqs,qkgd->skd",
        probs.astype(jnp.bfloat16),
        grad_grouped,
        preferred_element_type=jnp.float32,
    )
    grad_probs = jnp.einsum(
        "qkgd,skd->kgqs", grad_grouped, value_low, preferred_element_type=jnp.float32
    )
    centre = jnp.sum(probs * grad_probs, axis=-1, keepdims=True)
    grad_scores = (probs * (grad_probs - centre)).astype(jnp.bfloat16)
    grad_query = (
        jnp.einsum("kgqs,skd->qkgd", grad_scores, key_rot, preferred_element_type=jnp.float32)
        * scale
    )
    grad_key = (
        jnp.einsum("kgqs,qkgd->skd", grad_scores, grouped, preferred_element_type=jnp.float32)
        * scale
    )
    cosine, sine = angles(seg_row)
    grad_query = unrotate(grad_query.reshape(length, -1, HD), cosine, sine)
    grad_key = unrotate(grad_key, cosine, sine)
    return (
        grad_query.reshape(length, -1).astype(jnp.bfloat16),
        grad_key.reshape(length, -1).astype(jnp.bfloat16),
        grad_value.reshape(length, -1).astype(jnp.bfloat16),
    )


MESH = pl.DeviceIdType.MESH
VMEM_ASK = 56 * 1024 * 1024


def flip(index, bit):
    return index + bit - 2 * bit * ((index // bit) % 2)


def orders_of(size):
    bits = [1 << k for k in range(size.bit_length() - 1)]
    rest = bits[1:]
    cut = len(rest) // 2
    near, far = rest[:cut], rest[cut:]
    return [bits[:1] + near + far, bits[:1] + far + near]


def flip_any(index, mask):
    bit = 1
    while bit <= mask:
        if mask & bit:
            index = flip(index, bit)
        bit *= 2
    return index


def greet_cube(axis, me, size):
    barrier = pltpu.get_barrier_semaphore()
    bits = [1 << k for k in range(size.bit_length() - 1)]
    for bit in bits:
        pl.semaphore_signal(barrier, inc=1, device_id={axis: flip(me, bit)}, device_id_type=MESH)
    pl.semaphore_wait(barrier, len(bits))


def gather_kernel(axis, size, count, *refs):
    ins, outs, sems = refs[:count], refs[count : 2 * count], refs[2 * count :]
    me = lax.axis_index(axis)
    greet_cube(axis, me, size)
    for a in range(count):
        outs[a][me] = ins[a][...]
    orders = [order[::-1] for order in orders_of(size)]
    held = [[0], [0]]
    for phase in range(len(orders[0])):
        copies = []
        for a in range(count):
            half = ins[a].shape[0] // 2
            for part in range(2):
                bit = orders[part][phase]
                for mask in held[part]:
                    view = outs[a].at[flip_any(me, mask), pl.ds(part * half, half)]
                    copies.append(
                        pltpu.make_async_remote_copy(
                            src_ref=view,
                            dst_ref=view,
                            send_sem=sems[0].at[a, part, mask | bit],
                            recv_sem=sems[1].at[a, part, mask | bit],
                            device_id={axis: flip(me, bit)},
                            device_id_type=MESH,
                        )
                    )
        for copy in copies:
            copy.start()
        for copy in copies:
            copy.wait()
        held = [
            held[part] + [mask | orders[part][phase] for mask in held[part]] for part in range(2)
        ]


def params(number):
    return pltpu.CompilerParams(
        collective_id=number, has_side_effects=True, vmem_limit_bytes=VMEM_ASK
    )


def cost(byte_count):
    return pl.CostEstimate(flops=0, bytes_accessed=byte_count, transcendentals=0)


def cube_gather(arrays, axis, number):
    size = lax.axis_size(axis)
    count = len(arrays)
    return pl.pallas_call(
        functools.partial(gather_kernel, axis, size, count),
        out_shape=[jax.ShapeDtypeStruct((size,) + a.shape, a.dtype) for a in arrays],
        in_specs=[pl.BlockSpec(memory_space=pltpu.VMEM)] * count,
        out_specs=[pl.BlockSpec(memory_space=pltpu.VMEM)] * count,
        scratch_shapes=[pltpu.SemaphoreType.DMA((count, 2, size))] * 2,
        compiler_params=params(number),
        cost_estimate=cost(60000000),
        name="cube_gather",
    )(*arrays)


def scatter_kernel(axis, size, count, *refs):
    ins, outs = refs[:count], refs[count : 2 * count]
    got, keep = refs[2 * count : 3 * count], refs[3 * count : 4 * count]
    sems = refs[4 * count :]
    me = lax.axis_index(axis)
    greet_cube(axis, me, size)
    orders = orders_of(size)
    live = [list(range(size)), list(range(size))]
    phases = len(orders[0])
    for phase in range(phases):
        copies = []
        for a in range(count):
            half = outs[a].shape[0] // 2
            for part in range(2):
                bit = orders[part][phase]
                rows = pl.ds(part * half, half)
                for mask in live[part]:
                    if not mask & bit:
                        continue
                    if phase == 0:
                        source = ins[a].at[flip_any(me, mask), rows]
                    else:
                        source = keep[a].at[mask // 2, rows]
                    copies.append(
                        pltpu.make_async_remote_copy(
                            src_ref=source,
                            dst_ref=got[a].at[mask, rows],
                            send_sem=sems[0].at[a, part, mask],
                            recv_sem=sems[1].at[a, part, mask],
                            device_id={axis: flip(me, bit)},
                            device_id_type=MESH,
                        )
                    )
        for copy in copies:
            copy.start()
        for copy in copies:
            copy.wait()
        for a in range(count):
            half = outs[a].shape[0] // 2
            for part in range(2):
                bit = orders[part][phase]
                rows = pl.ds(part * half, half)
                stay = [mask for mask in live[part] if not mask & bit]
                for mask in stay:
                    if phase == 0:
                        own = ins[a][flip_any(me, mask), rows]
                    else:
                        own = keep[a][mask // 2, rows]
                    total = own.astype(jnp.float32) + got[a][mask | bit, rows].astype(jnp.float32)
                    if phase == phases - 1:
                        outs[a][rows] = total
                    else:
                        keep[a][mask // 2, rows] = total.astype(keep[a].dtype)
        live = [[m for m in live[part] if not m & orders[part][phase]] for part in range(2)]


def cube_scatter(arrays, axis, number):
    size = lax.axis_size(axis)
    count = len(arrays)
    slots = [pltpu.VMEM(a.shape, a.dtype) for a in arrays]
    return pl.pallas_call(
        functools.partial(scatter_kernel, axis, size, count),
        out_shape=[jax.ShapeDtypeStruct(a.shape[1:], jnp.float32) for a in arrays],
        in_specs=[pl.BlockSpec(memory_space=pltpu.VMEM)] * count,
        out_specs=[pl.BlockSpec(memory_space=pltpu.VMEM)] * count,
        scratch_shapes=slots
        + [pltpu.VMEM((size // 2,) + a.shape[1:], a.dtype) for a in arrays]
        + [pltpu.SemaphoreType.DMA((count, 2, size))] * 2,
        compiler_params=params(number),
        cost_estimate=cost(60000000),
        name="cube_scatter",
    )(*arrays)


def greet_line(axis, me, size):
    barrier = pltpu.get_barrier_semaphore()
    for ok, other in ((me < size - 1, me + 1), (me > 0, me - 1)):

        @pl.when(ok)
        def _(other=other):
            pl.semaphore_signal(barrier, inc=1, device_id={axis: other}, device_id_type=MESH)

    inner = (me < size - 1) & (me > 0)

    @pl.when(inner)
    def _():
        pl.semaphore_wait(barrier, 2)

    @pl.when(jnp.logical_not(inner))
    def _():
        pl.semaphore_wait(barrier, 1)


def line_gather_kernel(axis, size, x_ref, out_ref, send_sem, recv_sem):
    me = lax.axis_index(axis)
    greet_line(axis, me, size)
    out_ref[me] = x_ref[...]

    def copy_of(way, step, block, target):
        return pltpu.make_async_remote_copy(
            src_ref=out_ref.at[block],
            dst_ref=out_ref.at[block],
            send_sem=send_sem.at[way, step],
            recv_sem=recv_sem.at[way, step],
            device_id={axis: target},
            device_id_type=MESH,
        )

    for step in range(size - 1):

        @pl.when((me - step >= 0) & (me < size - 1))
        def _(step=step):
            copy_of(0, step, me - step, me + 1).start()

        @pl.when((me + step <= size - 1) & (me > 0))
        def _(step=step):
            copy_of(1, step, me + step, me - 1).start()

        @pl.when(me - 1 - step >= 0)
        def _(step=step):
            copy_of(0, step, me - 1 - step, me - 1).wait_recv()

        @pl.when(me + 1 + step <= size - 1)
        def _(step=step):
            copy_of(1, step, me + 1 + step, me + 1).wait_recv()

    for step in range(size - 1):

        @pl.when((me - step >= 0) & (me < size - 1))
        def _(step=step):
            copy_of(0, step, me - step, me + 1).wait_send()

        @pl.when((me + step <= size - 1) & (me > 0))
        def _(step=step):
            copy_of(1, step, me + step, me - 1).wait_send()


def line_gather(array, axis, number):
    size = lax.axis_size(axis)
    return pl.pallas_call(
        functools.partial(line_gather_kernel, axis, size),
        out_shape=jax.ShapeDtypeStruct((size,) + array.shape, array.dtype),
        in_specs=[pl.BlockSpec(memory_space=pltpu.VMEM)],
        out_specs=pl.BlockSpec(memory_space=pltpu.VMEM),
        scratch_shapes=[pltpu.SemaphoreType.DMA((2, size))] * 2,
        compiler_params=params(number),
        cost_estimate=cost(80000000),
        name="line_gather",
    )(array)


def line_scatter_kernel(axis, size, x_ref, out_ref, stage, got, send_sem, recv_sem):
    me = lax.axis_index(axis)
    greet_line(axis, me, size)

    def copy_of(way, dest, target):
        return pltpu.make_async_remote_copy(
            src_ref=stage.at[way, dest],
            dst_ref=got.at[way, dest],
            send_sem=send_sem.at[way, dest],
            recv_sem=recv_sem.at[way, dest],
            device_id={axis: target},
            device_id_type=MESH,
        )

    def pass_on(way, dest, source, target, first):
        @pl.when(first)
        def _():
            stage[way, dest] = x_ref[dest]

        @pl.when(jnp.logical_not(first))
        def _():
            copy_of(way, dest, source).wait_recv()
            stage[way, dest] = (
                x_ref[dest].astype(jnp.float32) + got[way, dest].astype(jnp.float32)
            ).astype(stage.dtype)

        copy_of(way, dest, target).start()

    for k in range(size - 1):
        up, down = size - 1 - k, k

        @pl.when(me < up)
        def _(up=up):
            pass_on(0, up, me - 1, me + 1, me == 0)

        @pl.when(me > down)
        def _(down=down):
            pass_on(1, down, me + 1, me - 1, me == size - 1)

    out_ref[...] = x_ref[me].astype(jnp.float32)

    @pl.when(me > 0)
    def _():
        copy_of(0, me, me - 1).wait_recv()
        out_ref[...] += got[0, me].astype(jnp.float32)

    @pl.when(me < size - 1)
    def _():
        copy_of(1, me, me + 1).wait_recv()
        out_ref[...] += got[1, me].astype(jnp.float32)

    for k in range(size - 1):
        up, down = size - 1 - k, k

        @pl.when(me < up)
        def _(up=up):
            copy_of(0, up, me + 1).wait_send()

        @pl.when(me > down)
        def _(down=down):
            copy_of(1, down, me - 1).wait_send()


def line_scatter(array, axis, number):
    size = lax.axis_size(axis)
    return pl.pallas_call(
        functools.partial(line_scatter_kernel, axis, size),
        out_shape=jax.ShapeDtypeStruct(array.shape[1:], jnp.float32),
        in_specs=[pl.BlockSpec(memory_space=pltpu.VMEM)],
        out_specs=pl.BlockSpec(memory_space=pltpu.VMEM),
        scratch_shapes=[pltpu.VMEM((2,) + array.shape, array.dtype)] * 2
        + [pltpu.SemaphoreType.DMA((2, size))] * 2,
        compiler_params=params(number),
        cost_estimate=cost(80000000),
        name="line_scatter",
    )(array)


def total_kernel(sizes, x_ref, out_ref, got, sent, send_sem, recv_sem):
    steps = []
    for axis, size in sizes:
        steps += [(axis, 1 << k) for k in range(size.bit_length() - 1)]
    barrier = pltpu.get_barrier_semaphore()
    for axis, bit in steps:
        pl.semaphore_signal(
            barrier,
            inc=1,
            device_id={axis: flip(lax.axis_index(axis), bit)},
            device_id_type=MESH,
        )
    pl.semaphore_wait(barrier, len(steps))
    sent[0] = x_ref[...]
    for k, (axis, bit) in enumerate(steps):
        copy = pltpu.make_async_remote_copy(
            src_ref=sent.at[k],
            dst_ref=got.at[k],
            send_sem=send_sem.at[k],
            recv_sem=recv_sem.at[k],
            device_id={axis: flip(lax.axis_index(axis), bit)},
            device_id_type=MESH,
        )
        copy.start()
        copy.wait()
        if k == len(steps) - 1:
            out_ref[...] = sent[k] + got[k]
        else:
            sent[k + 1] = sent[k] + got[k]


def total_of(array, axes, number):
    sizes = [(axis, lax.axis_size(axis)) for axis in axes]
    count = sum(size.bit_length() - 1 for _, size in sizes)
    return pl.pallas_call(
        functools.partial(total_kernel, sizes),
        out_shape=jax.ShapeDtypeStruct(array.shape, array.dtype),
        in_specs=[pl.BlockSpec(memory_space=pltpu.VMEM)],
        out_specs=pl.BlockSpec(memory_space=pltpu.VMEM),
        scratch_shapes=[pltpu.VMEM((count,) + array.shape, array.dtype)] * 2
        + [pltpu.SemaphoreType.DMA((count,))] * 2,
        compiler_params=params(number),
        cost_estimate=cost(60000000),
        name="total",
    )(array)


def local(
    block_in,
    segments,
    routes,
    attn_gain,
    w_query,
    w_key,
    w_value,
    w_out,
    moe_gain,
    w_router,
    w_gate_up,
    w_down,
    grad_out,
):
    dp_size = lax.axis_size("dp")
    mp_index = lax.axis_index("mp")
    dp_index = lax.axis_index("dp")
    tok_dev = routes.shape[0]
    seqs_here = segments.shape[0]
    exp_dev = EXPERTS // dp_size
    stacked = line_gather(block_in, "mp", 1)
    stacked, w_gate_up, w_down = lax.optimization_barrier((stacked, w_gate_up, w_down))
    gate_up = lax.all_gather(w_gate_up, "mp", axis=2, tiled=True)
    down_full = lax.all_gather(w_down, "mp", axis=2, tiled=True)
    full_rows = stacked.transpose(1, 0, 2).reshape(block_in.shape[0], -1)
    row_count = full_rows.shape[0]
    length = row_count // seqs_here
    wide = full_rows.astype(jnp.float32)
    normed_low = rms_scale(wide, attn_gain).astype(jnp.bfloat16)
    q_cols, k_cols = w_query.shape[1], w_key.shape[1]
    packed = jnp.concatenate([w_query, w_key, w_value, w_out], axis=1)
    (gathered,) = cube_gather([packed], "dp", 2)
    gathered = gathered.reshape(-1, packed.shape[1])
    qkv_cols = q_cols + 2 * k_cols
    qkv_full = gathered[:, :qkv_cols]
    out_part = gathered[:, qkv_cols:]
    qkv = jnp.dot(normed_low, qkv_full, preferred_element_type=jnp.float32)
    query = qkv[:, :q_cols]
    key = qkv[:, q_cols : q_cols + k_cols]
    value = qkv[:, q_cols + k_cols :]
    head_local = q_cols // HD
    kv_local = k_cols // HD
    mixed, log_total, query_rot, key_rot, value_low = lax.map(
        attend_forward,
        (
            query.reshape(seqs_here, length, head_local, HD),
            key.reshape(seqs_here, length, kv_local, HD),
            value.reshape(seqs_here, length, kv_local, HD),
            segments,
        ),
    )
    heads_low = mixed.reshape(row_count, head_local * HD)
    row_start = mp_index * tok_dev
    attn_mixed = line_scatter(
        jnp.einsum("rh,dh->rd", heads_low, out_part, preferred_element_type=jnp.float32)
        .astype(jnp.bfloat16)
        .reshape(-1, tok_dev, D),
        "mp",
        3,
    )
    own_rows = lax.dynamic_slice_in_dim(wide, row_start, tok_dev, 0)
    hidden = own_rows + attn_mixed
    moe_low = rms_scale(hidden, moe_gain).astype(jnp.bfloat16)
    logits = jnp.dot(moe_low, w_router, preferred_element_type=jnp.float32)
    used = jnp.sum(
        (routes[:, :, None] == jnp.arange(EXPERTS, dtype=jnp.int32)[None, None, :]).astype(
            jnp.float32
        ),
        axis=1,
    )
    routed = used > 0.0
    top_logit = jnp.max(jnp.where(routed, logits, NEG_FILL), axis=1, keepdims=True)
    raised = jnp.where(routed, jnp.exp(jnp.where(routed, logits - top_logit, 0.0)), 0.0)
    gates = raised / jnp.sum(raised, axis=1, keepdims=True)
    order = jnp.arange(tok_dev, dtype=jnp.int32)
    before = (order[:, None] > order[None, :]).astype(jnp.bfloat16)
    rank = jnp.dot(before, used.astype(jnp.bfloat16), preferred_element_type=jnp.float32)
    rank = jnp.where(routed, rank, -1.0)
    info = jnp.concatenate(
        [gates, rank, jnp.zeros((tok_dev, 128 - 2 * EXPERTS), jnp.float32)], axis=1
    )
    tokens, tops, infos = cube_gather([moe_low, grad_out, info], "dp", 4)
    first = dp_index * exp_dev
    gate_cols = lax.dynamic_slice_in_dim(infos, first, exp_dev, 2)
    rank_cols = lax.dynamic_slice_in_dim(infos, EXPERTS + first, exp_dev, 2)
    gate_cols = gate_cols.transpose(0, 2, 1)
    rank_cols = rank_cols.transpose(0, 2, 1)
    place = jnp.arange(CAP, dtype=jnp.float32)[None, None, :, None]
    picks_wide = rank_cols[:, :, None, :] == place
    picks = picks_wide.astype(jnp.bfloat16)
    slot_gates = jnp.sum(jnp.where(picks_wide, gate_cols[:, :, None, :], 0.0), axis=3)
    arrived = jnp.einsum(
        "sect,std->secd", picks, tokens, preferred_element_type=jnp.float32
    ).astype(jnp.bfloat16)
    top_rows = jnp.einsum("sect,std->secd", picks, tops, preferred_element_type=jnp.float32)
    grad_arrived = (slot_gates[..., None] * top_rows).astype(jnp.bfloat16)
    both = jnp.einsum("secd,edf->secf", arrived, gate_up, preferred_element_type=jnp.float32)
    gate_part = both[..., :FF]
    up_part = both[..., FF:]
    act_low = (jax.nn.silu(gate_part) * up_part).astype(jnp.bfloat16)
    expert_out = jnp.einsum(
        "secf,efd->secd", act_low, down_full, preferred_element_type=jnp.float32
    ).astype(jnp.bfloat16)
    grad_slots = jnp.sum(top_rows * expert_out.astype(jnp.float32), axis=3)
    scaled_out = (slot_gates[..., None] * expert_out.astype(jnp.float32)).astype(jnp.bfloat16)
    part_out = jnp.einsum(
        "sect,secd->std", picks, scaled_out, preferred_element_type=jnp.float32
    ).astype(jnp.bfloat16)
    grad_act = jnp.einsum(
        "secd,efd->secf", grad_arrived, down_full, preferred_element_type=jnp.float32
    )
    grad_down = jnp.einsum(
        "secf,secd->efd", act_low, grad_arrived, preferred_element_type=jnp.float32
    )
    grad_down = lax.psum_scatter(
        grad_down.astype(jnp.bfloat16), "mp", scatter_dimension=2, tiled=True
    ).astype(jnp.float32)
    sigma = jax.nn.sigmoid(gate_part)
    grad_gate = grad_act * up_part * sigma * (1.0 + gate_part * (1.0 - sigma))
    grad_up = grad_act * gate_part * sigma
    grad_both = jnp.concatenate([grad_gate, grad_up], axis=-1).astype(jnp.bfloat16)
    grad_gate_up = jnp.einsum(
        "secd,secf->edf", arrived, grad_both, preferred_element_type=jnp.float32
    )
    grad_copy = jnp.einsum(
        "secf,edf->secd", grad_both, gate_up, preferred_element_type=jnp.float32
    ).astype(jnp.bfloat16)
    part_moe = jnp.einsum(
        "sect,secd->std", picks, grad_copy, preferred_element_type=jnp.float32
    ).astype(jnp.bfloat16)
    part_gates = jnp.sum(jnp.where(picks_wide, grad_slots[..., None], 0.0), axis=2)
    part_gates = lax.dynamic_update_slice_in_dim(
        jnp.zeros((dp_size, tok_dev, 128), jnp.float32), part_gates.transpose(0, 2, 1), first, 2
    )
    moe_sum, grad_gates = cube_scatter([part_moe, part_gates], "dp", 5)
    (out_sum,) = cube_scatter([part_out], "dp", 6)
    block_out = (hidden + out_sum).astype(jnp.bfloat16)
    grad_gates = grad_gates[:, :EXPERTS]
    grad_top = grad_out.astype(jnp.float32)
    grad_logits = gates * (grad_gates - jnp.sum(gates * grad_gates, axis=1, keepdims=True))
    router_wide = w_router.astype(jnp.float32)
    grad_moe = moe_sum + jnp.einsum("te,de->td", grad_logits, router_wide, precision=HIGH)
    grad_router = jnp.einsum("td,te->ed", moe_low.astype(jnp.float32), grad_logits, precision=HIGH)
    unused, moe_pull = jax.vjp(rms_scale, hidden, moe_gain)
    grad_hidden, grad_moe_gain = moe_pull(grad_moe)
    grad_hidden = grad_hidden + grad_top
    grad_hidden_low = grad_hidden.astype(jnp.bfloat16)
    grad_full = line_gather(grad_hidden_low, "mp", 7)
    grad_full, grad_gate_up = lax.optimization_barrier(
        (grad_full, grad_gate_up.astype(jnp.bfloat16))
    )
    grad_full = grad_full.reshape(row_count, D)
    grad_gate_up = lax.psum_scatter(
        grad_gate_up, "mp", scatter_dimension=2, tiled=True
    ).astype(jnp.float32)
    grad_heads = jnp.dot(grad_full, out_part, preferred_element_type=jnp.float32).astype(
        jnp.bfloat16
    )
    grad_out_w = jnp.einsum("rd,rh->dh", grad_full, heads_low, preferred_element_type=jnp.float32)
    grad_query, grad_key, grad_value = lax.map(
        attend_backward,
        (
            grad_heads.reshape(seqs_here, length, head_local * HD),
            query_rot,
            key_rot,
            value_low,
            log_total,
            segments,
        ),
    )
    grad_qkv = jnp.concatenate(
        [
            grad_query.reshape(row_count, q_cols),
            grad_key.reshape(row_count, k_cols),
            grad_value.reshape(row_count, k_cols),
        ],
        axis=1,
    )
    grad_normed = line_scatter(
        jnp.einsum("rh,dh->rd", grad_qkv, qkv_full, preferred_element_type=jnp.float32)
        .astype(jnp.bfloat16)
        .reshape(-1, tok_dev, D),
        "mp",
        8,
    )
    unused_two, attn_pull = jax.vjp(rms_scale, own_rows, attn_gain)
    grad_own, grad_attn_gain = attn_pull(grad_normed)
    grad_in = grad_own + grad_hidden
    grad_qkv_w = jnp.einsum("rd,rh->dh", normed_low, grad_qkv, preferred_element_type=jnp.float32)
    grad_w = jnp.concatenate([grad_qkv_w, grad_out_w], axis=1).astype(jnp.bfloat16)
    (grad_w,) = cube_scatter([grad_w.reshape(dp_size, -1, grad_w.shape[1])], "dp", 9)
    small = jnp.concatenate(
        [
            grad_router,
            grad_attn_gain[None, :],
            grad_moe_gain[None, :],
            jnp.zeros((6, D), jnp.float32),
        ],
        axis=0,
    )
    small = total_of(small, ("dp", "mp"), 10)
    return (
        block_out,
        grad_in,
        small[EXPERTS],
        grad_w[:, :q_cols],
        grad_w[:, q_cols : q_cols + k_cols],
        grad_w[:, q_cols + k_cols : qkv_cols],
        grad_w[:, qkv_cols:],
        small[EXPERTS + 1],
        small[:EXPERTS].T,
        grad_gate_up,
        grad_down,
    )


def solution(mesh):
    placed = (
        P("dp", "mp"),
        P("dp", None),
        P(("dp", "mp"), None),
        P(),
        P("dp", "mp"),
        P("dp", "mp"),
        P("dp", "mp"),
        P("dp", "mp"),
        P(),
        P(),
        P("dp", None, "mp"),
        P("dp", None, "mp"),
        P(("dp", "mp"), None),
    )
    return jax.shard_map(
        local,
        mesh=mesh,
        in_specs=placed,
        out_specs=(
            P(("dp", "mp"), None),
            P(("dp", "mp"), None),
            P(),
            P("dp", "mp"),
            P("dp", "mp"),
            P("dp", "mp"),
            P("dp", "mp"),
            P(),
            P(),
            P("dp", None, "mp"),
            P("dp", None, "mp"),
        ),
        check_vma=False,
    )
```
